32 devices in a mesh: section: 4 (over x, core), lat: 4 (over z), lon: 2 (over y).
Axes of the slice: x: 2, y: 2, z: 4, core: 2. Of those that a mesh axis runs over, the one named last changes fastest.
Arguments:
- states: bfloat16 [4, 1, 96, 24, 192], P('section', None, 'lat', 'lon'), may hold values from -60 to 60
- loss_grads: bfloat16 [4, 1, 96, 24, 192], P('section', None, 'lat', 'lon'), may hold values from -6 to 6
- land_sea: int32 [96, 24], P('lat', 'lon'), may hold values 0 or 1
- land_embed: float32 [192], replicated, may hold values from -4 to 4
- gain_attn: float32 [192], replicated, may hold values from 0.5 to 1.5
- gain_mlp: float32 [192], replicated, may hold values from 0.5 to 1.5
- w_qkv: bfloat16 [192, 576], replicated, may hold values from -0.4375 to 0.4375
- w_out: bfloat16 [192, 192], replicated, may hold values from -0.4375 to 0.4375
- w_up: bfloat16 [192, 768], replicated, may hold values from -0.4375 to 0.4375
- w_down: bfloat16 [768, 192], replicated, may hold values from -0.21875 to 0.21875
Outputs:
- state_grads: float32 [4, 1, 96, 24, 192], P('section', None, 'lat', 'lon')
- grad_qkv: float32 [192, 576], replicated
- grad_out: float32 [192, 192], replicated
- grad_up: float32 [192, 768], replicated
- grad_down: float32 [768, 192], replicated
- grad_land: float32 [192], replicated
- grad_gain_attn: float32 [192], replicated
- grad_gain_mlp: float32 [192], replicated
The draws below stay inside these ranges and needn't reach their ends.
All inputs are finite; a program needn't handle non-finite values. No bound on the sum of `land_sea` on one device may be relied on, other than what follows from the above.
Results may differ from the reference program's by a relative error of at most 0.015.
Values may be sent and summed in bfloat16 or wider, within the bound.
A program may use at most 64 MiB of HBM per device.

```python
import math
import jax
import jax.numpy as jnp
from jax import lax

CHANNELS = 192
HEADS = 6
MLP_WIDTH = 768
HEAD_DIM = 32
LEVELS = 1
WIN_LAT = 6
WIN_LON = 12
SECTIONS = 4
LAT_ALL = 96
LON_ALL = 24


def draw_states(key, part):
    key = jax.random.fold_in(key, 11)
    chan_key, token_key, base_key = jax.random.split(key, 3)
    shape = (SECTIONS, LEVELS, LAT_ALL, LON_ALL, CHANNELS)
    channel_scale = jnp.exp(jax.random.uniform(chan_key, (CHANNELS,), jnp.float32, math.log(0.3), math.log(3.0)))
    token_scale = jnp.exp(jax.random.uniform(token_key, (SECTIONS, LEVELS, LAT_ALL, LON_ALL, 1), jnp.float32, math.log(0.5), math.log(5.0)))
    base = jnp.clip(jax.random.normal(base_key, shape, jnp.float32), -4.0, 4.0)
    return (base * channel_scale * token_scale).astype(jnp.bfloat16)


def place_ends(drawn, rng, least, high):
    index_at = [jax.random.randint(jax.random.fold_in(rng, axis), (), 0, length) for axis, length in enumerate(drawn.shape)]
    longest = drawn.shape.index(max(drawn.shape))
    next_to = index_at[:longest] + [(index_at[longest] + 1) % drawn.shape[longest]] + index_at[longest + 1:]
    return drawn.at[tuple(index_at)].set(least).at[tuple(next_to)].set(high)


def levels(rng, dims, shards, smallest, top_value):
    level = 1.0
    for dim, parts in shards:
        heights = jax.random.uniform(jax.random.fold_in(jax.random.fold_in(rng, 6), dim), (parts,), jnp.float32, smallest / len(shards), top_value / len(shards))
        level = level * jnp.repeat(jnp.exp(heights), dims[dim] // parts).reshape((-1,) + (1,) * (len(dims) - 1 - dim))
    return level


def normal_values(stream_key, dims, deviation, limit, pieces=(), kind=jnp.bfloat16):
    entries = deviation * jax.random.normal(stream_key, dims, jnp.float32)
    if pieces:
        entries = entries * levels(stream_key, dims, pieces, -0.22, 0.18)
    return jnp.clip(entries, -limit, limit).astype(kind)


def setup_inputs(seed: int = 0) -> dict:
    splits = jax.random.split(jax.random.key(seed), 11)
    return {
        "states": draw_states(jax.random.fold_in(splits[10], 71), 0),
        "loss_grads": normal_values(splits[1], (SECTIONS, LEVELS, LAT_ALL, LON_ALL, CHANNELS), 1.0, 6.0, ((0, 4), (2, 4), (3, 2))),
        "land_sea": place_ends((jax.random.randint(splits[2], (LAT_ALL, LON_ALL), 0, 10) < 3).astype(jnp.int32), jax.random.fold_in(splits[2], 1), 0, 1),
        "land_embed": normal_values(splits[3], (CHANNELS,), 1.0, 4.0, (), jnp.float32),
        "gain_attn": jnp.clip(1.0 + 0.1 * jax.random.normal(splits[4], (CHANNELS,), jnp.float32), 0.5, 1.5),
        "gain_mlp": jnp.clip(1.0 + 0.1 * jax.random.normal(splits[5], (CHANNELS,), jnp.float32), 0.5, 1.5),
        "w_qkv": normal_values(splits[6], (CHANNELS, 3 * CHANNELS), CHANNELS ** -0.5, 0.4375),
        "w_out": normal_values(splits[7], (CHANNELS, CHANNELS), CHANNELS ** -0.5, 0.4375),
        "w_up": normal_values(splits[8], (CHANNELS, MLP_WIDTH), CHANNELS ** -0.5, 0.4375),
        "w_down": normal_values(splits[9], (MLP_WIDTH, CHANNELS), MLP_WIDTH ** -0.5, 0.21875),
    }


EPS = 1e-05

def normalize(field, gain):
    centre = lax.optimization_barrier(jnp.mean(field, axis=-1, keepdims=True))
    offset = field - centre
    spread = lax.optimization_barrier(jnp.mean(offset * offset, axis=-1, keepdims=True))
    return offset * lax.rsqrt(spread + EPS) * gain

def exact_gelu(values):
    return jax.nn.gelu(values, approximate=False)

def to_windows(field):
    depth, height, breadth, width = field.shape
    grid = field.reshape(depth, height // WIN_LAT, WIN_LAT, breadth // WIN_LON, WIN_LON, width)
    grid = grid.transpose(1, 3, 0, 2, 4, 5)
    return grid.reshape(height // WIN_LAT, breadth // WIN_LON, depth * WIN_LAT * WIN_LON, width)

def from_windows(blocks, depth):
    band_count, cell_count, tokens, width = blocks.shape
    grid = blocks.reshape(band_count, cell_count, depth, WIN_LAT, WIN_LON, width)
    grid = grid.transpose(2, 0, 3, 1, 4, 5)
    return grid.reshape(depth, band_count * WIN_LAT, cell_count * WIN_LON, width)

def allowed_pairs(first_row, total_rows, band_count, depth):
    row_ids = first_row + jnp.arange(band_count * WIN_LAT, dtype=jnp.int32)
    source = (row_ids + WIN_LAT // 2) % total_rows
    labels = (source < WIN_LAT // 2).astype(jnp.int32).reshape(band_count, 1, WIN_LAT, 1)
    labels = jnp.broadcast_to(labels, (band_count, depth, WIN_LAT, WIN_LON))
    labels = labels.reshape(band_count, depth * WIN_LAT * WIN_LON)
    return (labels[:, :, None] == labels[:, None, :]).astype(jnp.float32)

def heads_of(block):
    band_count, cell_count, tokens, width = block.shape
    return block.reshape(band_count, cell_count, tokens, HEADS, width // HEADS)

def merge_heads(block):
    band_count, cell_count, tokens, heads, size = block.shape
    return block.reshape(band_count, cell_count, tokens, heads * size)

def attend(qkv_win, allow):
    width = qkv_win.shape[-1] // 3
    query = heads_of(qkv_win[..., :width]).astype(jnp.float32)
    keys = heads_of(qkv_win[..., width:2 * width]).astype(jnp.float32)
    values = heads_of(qkv_win[..., 2 * width:]).astype(jnp.float32)
    scores = jnp.einsum('abqhd,abkhd->abhqk', query, keys) * HEAD_DIM ** (-0.5)
    weights = jnp.exp(scores) * allow[:, None, None]
    probs = weights / lax.optimization_barrier(jnp.sum(weights, axis=-1, keepdims=True))
    rounded = lax.optimization_barrier(probs.astype(jnp.bfloat16)).astype(jnp.float32)
    mixed = jnp.einsum('abhqk,abkhd->abqhd', rounded, values)
    return (probs, merge_heads(mixed).astype(jnp.bfloat16))

def attend_back(qkv_win, probs, d_mixed):
    width = qkv_win.shape[-1] // 3
    query = heads_of(qkv_win[..., :width]).astype(jnp.float32)
    keys = heads_of(qkv_win[..., width:2 * width]).astype(jnp.float32)
    values = heads_of(qkv_win[..., 2 * width:]).astype(jnp.float32)
    d_heads = heads_of(d_mixed).astype(jnp.float32)
    rounded = lax.optimization_barrier(probs.astype(jnp.bfloat16)).astype(jnp.float32)
    d_probs = jnp.einsum('abqhd,abkhd->abhqk', d_heads, values)
    d_values = jnp.einsum('abhqk,abqhd->abkhd', rounded, d_heads)
    d_scores = probs * (d_probs - lax.optimization_barrier(jnp.sum(probs * d_probs, axis=-1, keepdims=True))) * HEAD_DIM ** (-0.5)
    d_scores = lax.optimization_barrier(d_scores.astype(jnp.bfloat16)).astype(jnp.float32)
    d_query = jnp.einsum('abhqk,abkhd->abqhd', d_scores, keys)
    d_keys = jnp.einsum('abhqk,abqhd->abkhd', d_scores, query)
    joined = jnp.concatenate([merge_heads(d_query), merge_heads(d_keys), merge_heads(d_values)], axis=-1)
    return joined.astype(jnp.bfloat16)

def attend_bands(qkv_win, allow):

    def one_band(item):
        probs, mixed = attend(item[0][None], item[1][None])
        return (probs[0], mixed[0])
    return lax.map(one_band, (qkv_win, allow))

def attend_back_bands(qkv_win, probs, d_mixed):

    def one_band(item):
        return attend_back(item[0][None], item[1][None], item[2][None])[0]
    return lax.map(one_band, (qkv_win, probs, d_mixed))

def roll_ahead(field):
    return jnp.roll(field, (-(WIN_LAT // 2), -(WIN_LON // 2)), axis=(1, 2))

def roll_behind(field):
    return jnp.roll(field, (WIN_LAT // 2, WIN_LON // 2), axis=(1, 2))

def section_backward(state, cotangent, land, land_embed, gain_attn, gain_mlp, w_qkv, w_out, w_up, w_down):
    depth, height, breadth, width = state.shape
    embedded = state.astype(jnp.float32) + land * land_embed
    normed, attn_back = jax.vjp(normalize, embedded, gain_attn)
    normed = normed.astype(jnp.bfloat16)
    rolled = roll_ahead(normed).reshape(-1, width)
    qkv = jnp.dot(rolled, w_qkv, preferred_element_type=jnp.float32).astype(jnp.bfloat16)
    qkv_win = to_windows(qkv.reshape(depth, height, breadth, 3 * width))
    allow = allowed_pairs(0, height, height // WIN_LAT, depth)
    probs, mixed_win = attend_bands(qkv_win, allow)
    mixed = from_windows(mixed_win, depth).reshape(-1, width)
    projected = jnp.dot(mixed, w_out, preferred_element_type=jnp.float32).astype(jnp.bfloat16)
    hidden_in = embedded + roll_behind(projected.reshape(depth, height, breadth, width)).astype(jnp.float32)
    normed_mlp, mlp_back = jax.vjp(normalize, hidden_in, gain_mlp)
    normed_mlp = normed_mlp.astype(jnp.bfloat16).reshape(-1, width)
    pre_act = jnp.dot(normed_mlp, w_up, preferred_element_type=jnp.float32)
    activated, gelu_back = jax.vjp(exact_gelu, pre_act)
    activated = activated.astype(jnp.bfloat16)
    cot_round = cotangent.astype(jnp.bfloat16).reshape(-1, width)
    grad_down = jnp.dot(activated.T, cot_round, preferred_element_type=jnp.float32)
    d_act = jnp.dot(cot_round, w_down.T, preferred_element_type=jnp.float32)
    d_pre = gelu_back(d_act)[0].astype(jnp.bfloat16)
    grad_up = jnp.dot(normed_mlp.T, d_pre, preferred_element_type=jnp.float32)
    d_normed_mlp = jnp.dot(d_pre, w_up.T, preferred_element_type=jnp.float32).reshape(depth, height, breadth, width)
    d_hidden, grad_gain_mlp = mlp_back(d_normed_mlp)
    d_hidden = cotangent + d_hidden
    d_projected = roll_ahead(d_hidden.astype(jnp.bfloat16)).reshape(-1, width)
    grad_out = jnp.dot(mixed.T, d_projected, preferred_element_type=jnp.float32)
    d_mixed = jnp.dot(d_projected, w_out.T, preferred_element_type=jnp.float32).astype(jnp.bfloat16)
    d_qkv_win = attend_back_bands(qkv_win, probs, to_windows(d_mixed.reshape(depth, height, breadth, width)))
    d_qkv = from_windows(d_qkv_win, depth).reshape(-1, 3 * width)
    grad_qkv = jnp.dot(rolled.T, d_qkv, preferred_element_type=jnp.float32)
    d_rolled = jnp.dot(d_qkv, w_qkv.T, preferred_element_type=jnp.float32).astype(jnp.bfloat16)
    d_normed = roll_behind(d_rolled.reshape(depth, height, breadth, width)).astype(jnp.float32)
    d_embedded, grad_gain_attn = attn_back(d_normed)
    d_state = d_hidden + d_embedded
    grad_land = lax.optimization_barrier(jnp.sum(d_state * land, axis=(0, 1, 2)))
    return (d_state, (grad_qkv, grad_out, grad_up, grad_down, grad_land, grad_gain_attn, grad_gain_mlp))

def reference(states, loss_grads, land_sea, land_embed, gain_attn, gain_mlp, w_qkv, w_out, w_up, w_down):
    land = land_sea.astype(jnp.float32)[None, :, :, None]
    incoming = jnp.zeros(states.shape[1:], jnp.float32)
    results = []
    totals = None
    for section_number in range(SECTIONS - 1, -1, -1):
        cotangent = loss_grads[section_number].astype(jnp.float32) + incoming
        d_state, grads = section_backward(states[section_number], cotangent, land, land_embed, gain_attn, gain_mlp, w_qkv, w_out, w_up, w_down)
        results.append(d_state)
        totals = grads if totals is None else jax.tree.map(jnp.add, totals, grads)
        incoming = lax.optimization_barrier(d_state.astype(jnp.bfloat16)).astype(jnp.float32)
    state_grads = jnp.stack(results[::-1])
    factor = float(SECTIONS * LEVELS * LAT_ALL * LON_ALL) ** (-0.5)
    return (state_grads, totals[0] * factor, totals[1] * factor, totals[2] * factor, totals[3] * factor, totals[4] * factor, totals[5] * factor, totals[6] * factor)
```

```python
import functools

import jax
import jax.numpy as jnp
from jax import lax
from jax.experimental import pallas as pl
from jax.experimental.pallas import tpu as pltpu
from jax.sharding import PartitionSpec as P

HEADS = 6
HEAD_DIM = 32
WIN_LAT = 6
WIN_LON = 12
WIDTH = 192
MLP = 768
EPS = 1e-05

HALF = (WIN_LAT // 2) * (WIN_LON // 2)
PAD = 24
MESH = pl.DeviceIdType.MESH
F32 = jnp.float32
BF16 = jnp.bfloat16


def dot_nn(a, b):
    return jnp.dot(a, b, preferred_element_type=F32)


def dot_nt(a, b):
    return lax.dot_general(a, b, (((1,), (1,)), ((), ())), preferred_element_type=F32)


def dot_tn(a, b):
    return lax.dot_general(a, b, (((0,), (0,)), ((), ())), preferred_element_type=F32)


def mean_last(v):
    return jnp.sum(v, axis=-1, keepdims=True) * (1.0 / v.shape[-1])


def norm_parts(v):
    offset = v - mean_last(v)
    scale = lax.rsqrt(mean_last(offset * offset) + EPS)
    return offset * scale, scale


def norm_back(d_out, gain, hat, scale):
    d_hat = d_out * gain
    return scale * (d_hat - mean_last(d_hat) - hat * mean_last(d_hat * hat))


def head_masks():
    lane = lax.broadcasted_iota(jnp.int32, (1, WIDTH), 1)
    return [(lane >= h * HEAD_DIM) & (lane < (h + 1) * HEAD_DIM) for h in range(HEADS)]


def spread_heads(block, masks):
    return jnp.concatenate([jnp.where(m, block, 0.0) for m in masks], axis=0).astype(BF16)


def join_heads(stacked, masks):
    rows = stacked.shape[0] // HEADS
    total = jnp.where(masks[0], stacked[:rows], 0.0)
    for h in range(1, HEADS):
        total = jnp.where(masks[h], stacked[h * rows : (h + 1) * rows], total)
    return total


def interleave(first, second, bands):
    span = 2 * PAD
    parts = []
    for b in range(bands):
        parts += [first[b * span : (b + 1) * span], second[b * span : (b + 1) * span]]
    return jnp.concatenate(parts, axis=0)


def separate(field, bands):
    span = 2 * PAD
    firsts = [field[2 * b * span : (2 * b + 1) * span] for b in range(bands)]
    seconds = [field[(2 * b + 1) * span : (2 * b + 2) * span] for b in range(bands)]
    return jnp.concatenate(firsts + seconds, axis=0)


def kernel(
    sizes,
    bands,
    chunk,
    factor,
    x_ref,
    loss_ref,
    land_ref,
    embed_ref,
    ga_ref,
    gm_ref,
    wqkv_ref,
    wout_ref,
    wup_ref,
    wdown_ref,
    d_state_ref,
    g_qkv_ref,
    g_out_ref,
    g_up_ref,
    g_down_ref,
    g_small_ref,
    halo_src,
    halo_edge,
    halo_diag,
    halo_side,
    qm_ref,
    k_ref,
    v_ref,
    pt_ref,
    emb_hat,
    hid_hat,
    cot_ref,
    cot_src,
    cot_in,
    gelu_ref,
    act_ref,
    nmlp_ref,
    rolled_ref,
    mixed_ref,
    dqkv_ref,
    grad_ref,
    grad_b,
    lon_in,
    lon_sum,
    lon_b,
    lat_in,
    lat_sum,
    lat_b,
    sec_in,
    gathered,
    halo_send,
    halo_recv,
    cot_send,
    cot_recv,
    rs_send,
    rs_recv,
    ag_send,
    ag_recv,
):
    n_sec, n_lat, n_lon = sizes
    sec = lax.axis_index("section")
    lat = lax.axis_index("lat")
    lon = lax.axis_index("lon")

    def there(d_sec, d_lat, d_lon):
        return (
            lax.rem(sec + d_sec + n_sec, n_sec),
            lax.rem(lat + d_lat + n_lat, n_lat),
            lax.rem(lon + d_lon + n_lon, n_lon),
        )

    peers = [(d, 0, 0) for d in range(1, n_sec)]
    peers += [(0, d, 0) for d in range(1, n_lat)]
    peers += [(0, 0, d) for d in range(1, n_lon)]
    peers += [(0, 1, 1), (0, -1, -1)]
    barrier = pltpu.get_barrier_semaphore()
    for peer in peers:
        pl.semaphore_signal(barrier, inc=1, device_id=there(*peer), device_id_type=MESH)
    pl.semaphore_wait(barrier, len(peers))

    half = 2 * bands * PAD

    def halo(number, sign, edge_row, diag_row, side_row):
        copies = []
        for kind, (src, dst, target) in enumerate(
            (
                (halo_src.at[number, pl.ds(edge_row, 32)], halo_edge.at[number], (0, sign, 0)),
                (halo_src.at[number, pl.ds(diag_row, 32)], halo_diag.at[number], (0, sign, sign)),
                (halo_src.at[number, pl.ds(side_row, half)], halo_side.at[number], (0, 0, sign)),
            )
        ):
            copy = pltpu.make_async_remote_copy(
                src_ref=src,
                dst_ref=dst,
                send_sem=halo_send.at[number, kind],
                recv_sem=halo_recv.at[number, kind],
                device_id=there(*target),
                device_id_type=MESH,
            )
            copy.start()
            copies.append(copy)
        return copies

    def start_ahead(number, field):
        halo_src[number] = field.astype(BF16)
        return halo(number, -1, half, 0, 0)

    def end_ahead(number, copies):
        for copy in copies:
            copy.wait_recv()
        own = halo_src[number, pl.ds(half, half)].astype(F32)
        edge = halo_edge[number].astype(F32)
        diag = halo_diag[number].astype(F32)
        side = halo_side[number].astype(F32)
        first = jnp.concatenate([own[PAD:], edge[:PAD]], axis=0)
        second = jnp.concatenate([side[PAD:], diag[:PAD]], axis=0)
        return interleave(first, second, bands).astype(BF16)

    def start_behind(number, field):
        halo_src[number] = separate(field, bands).astype(BF16)
        return halo(number, 1, half - 32, 2 * half - 32, half)

    def end_behind(number, copies):
        for copy in copies:
            copy.wait_recv()
        own = halo_src[number, pl.ds(0, half)].astype(F32)
        edge = halo_edge[number].astype(F32)
        diag = halo_diag[number].astype(F32)
        side = halo_side[number].astype(F32)
        return jnp.concatenate(
            [diag[32 - PAD :], side[: half - PAD], edge[32 - PAD :], own[: half - PAD]], axis=0
        )

    masks = head_masks()
    window = 4 * PAD
    root = HEAD_DIM ** (-0.5)
    land = land_ref[...]
    gain_attn = ga_ref[...]
    gain_mlp = gm_ref[...]

    embedded = x_ref[...].astype(F32) + land * embed_ref[...]
    hat, emb_scale = norm_parts(embedded)
    emb_hat[...] = hat
    ahead_fwd = start_ahead(0, hat * gain_attn)

    key_id = lax.broadcasted_iota(jnp.int32, (window, HEADS * window), 0)
    query_id = lax.broadcasted_iota(jnp.int32, (window, HEADS * window), 1)
    for h in range(1, HEADS):
        query_id = jnp.where(
            lax.broadcasted_iota(jnp.int32, (window, HEADS * window), 1) >= h * window,
            lax.broadcasted_iota(jnp.int32, (window, HEADS * window), 1) - h * window,
            query_id,
        )

    def block_of(ids):
        return [ids >= n * PAD for n in range(1, 4)]

    k1, k2, k3 = block_of(key_id)
    q1, q2, q3 = block_of(query_id)
    key_start = jnp.where(k3, 3 * PAD, jnp.where(k2, 2 * PAD, jnp.where(k1, PAD, 0)))
    valid = jnp.where(key_id - key_start < HALF, 1.0, 0.0)
    key_late = jnp.where(k3, 1.0, jnp.where(k2, 0.0, jnp.where(k1, 1.0, 0.0)))
    query_late = jnp.where(q3, 1.0, jnp.where(q2, 0.0, jnp.where(q1, 1.0, 0.0)))
    differ = (key_late - query_late) * (key_late - query_late)
    wraps = jnp.where(lat == n_lat - 1, 1.0, 0.0)
    valid_edge = valid * (1.0 - differ * wraps)

    rolled = end_ahead(0, ahead_fwd)
    rolled_ref[...] = rolled
    w_q = wqkv_ref[:, 0:WIDTH]
    w_k = wqkv_ref[:, WIDTH : 2 * WIDTH]
    w_v = wqkv_ref[:, 2 * WIDTH : 3 * WIDTH]
    query = dot_nn(rolled, w_q)
    keys = dot_nn(rolled, w_k).astype(BF16)
    values = dot_nn(rolled, w_v).astype(BF16)
    k_ref[...] = keys
    v_ref[...] = values
    mixes = []
    for b in range(bands):
        rows = slice(b * window, (b + 1) * window)
        q_heads = spread_heads(query[rows], masks)
        qm_ref[b] = q_heads
        scores = dot_nt(keys[rows], q_heads) * root
        weights = jnp.exp(scores) * (valid_edge if b == bands - 1 else valid)
        probs = weights / jnp.sum(weights, axis=0, keepdims=True)
        pt_ref[b] = probs
        mixes.append(join_heads(dot_tn(probs.astype(BF16), values[rows]), masks))
    mixed = jnp.concatenate(mixes, axis=0).astype(BF16)
    mixed_ref[...] = mixed
    behind_fwd = start_behind(1, dot_nn(mixed, wout_ref[...]))

    hidden = embedded + end_behind(1, behind_fwd)
    hat2, hid_scale = norm_parts(hidden)
    hid_hat[...] = hat2
    normed_mlp = (hat2 * gain_mlp).astype(BF16)
    nmlp_ref[...] = normed_mlp
    pre = dot_nn(normed_mlp, wup_ref[...])
    cdf = 0.5 + 0.5 * lax.erf(pre * (0.5**0.5))
    act_ref[...] = (pre * cdf).astype(BF16)
    gelu_ref[...] = cdf + pre * (jnp.exp(pre * pre * -0.5) * 0.3989422804014327)

    cot_ref[...] = loss_ref[...].astype(F32)
    cot_copy = pltpu.make_async_remote_copy(
        src_ref=cot_src,
        dst_ref=cot_in,
        send_sem=cot_send,
        recv_sem=cot_recv,
        device_id=there(-1, 0, 0),
        device_id_type=MESH,
    )

    @pl.when(sec < n_sec - 1)
    def _():
        cot_copy.wait_recv()
        cot_ref[...] += cot_in[...].astype(F32)

    cot = cot_ref[...]
    cot_round = cot.astype(BF16)
    d_pre = (gelu_ref[...] * dot_nt(cot_round, wdown_ref[...])).astype(BF16)
    d_nmlp = dot_nt(d_pre, wup_ref[...])
    d_hidden = cot + norm_back(d_nmlp, gain_mlp, hid_hat[...], hid_scale)
    ahead_bwd = start_ahead(2, d_hidden)

    def put_tiles(first, block):
        height = block.shape[0]
        for t in range(block.shape[1] // 128):
            start = (first + t) * height
            grad_ref[start : start + height, :] = block[:, t * 128 : (t + 1) * 128]

    def put_small(index, vector):
        row = 18 * WIDTH + 2 * index
        grad_ref[row : row + 1, :] = vector[:, :128]
        grad_ref[row + 1 : row + 2, 0:64] = vector[:, 128:WIDTH]

    small_rows = grad_ref.shape[0] - 18 * WIDTH
    grad_ref[18 * WIDTH :, :] = jnp.zeros((small_rows, 128), F32)
    put_tiles(6, dot_tn(nmlp_ref[...], d_pre))
    put_tiles(12, dot_tn(cot_round, act_ref[...]))
    put_small(2, jnp.sum(d_nmlp * hid_hat[...], axis=0, keepdims=True))

    d_projected = end_ahead(2, ahead_bwd)
    d_mixed = dot_nt(d_projected, wout_ref[...])
    d_queries, d_keys, d_values = [], [], []
    for b in range(bands):
        rows = slice(b * window, (b + 1) * window)
        d_heads = spread_heads(d_mixed[rows], masks)
        probs = pt_ref[b]
        d_probs = dot_nt(v_ref[rows, :], d_heads)
        weighted = probs * d_probs
        d_scores = (
            (weighted - probs * jnp.sum(weighted, axis=0, keepdims=True)) * root
        ).astype(BF16)
        d_values.append(dot_nn(probs.astype(BF16), d_heads))
        d_keys.append(dot_nn(d_scores, qm_ref[b]))
        d_queries.append(join_heads(dot_tn(d_scores, k_ref[rows, :]), masks))
    d_q = jnp.concatenate(d_queries, axis=0).astype(BF16)
    d_k = jnp.concatenate(d_keys, axis=0).astype(BF16)
    d_v = jnp.concatenate(d_values, axis=0).astype(BF16)
    d_rolled = dot_nt(d_q, w_q) + dot_nt(d_k, w_k) + dot_nt(d_v, w_v)
    behind_bwd = start_behind(3, d_rolled)

    rolled = rolled_ref[...]
    put_tiles(0, jnp.concatenate([dot_tn(rolled, d_q), dot_tn(rolled, d_k)], axis=1))
    put_tiles(
        3,
        jnp.concatenate([dot_tn(rolled, d_v), dot_tn(mixed_ref[...], d_projected)], axis=1),
    )

    d_normed = end_behind(3, behind_bwd)
    hat = emb_hat[...]
    d_state = d_hidden + norm_back(d_normed, gain_attn, hat, emb_scale)
    cot_src[...] = d_state.astype(BF16)

    @pl.when(sec > 0)
    def _():
        cot_copy.start()

    d_state_ref[...] = d_state
    put_small(0, jnp.sum(d_state * land, axis=0, keepdims=True))
    put_small(1, jnp.sum(d_normed * hat, axis=0, keepdims=True))

    waits = list(ahead_fwd + behind_fwd + ahead_bwd + behind_bwd)
    sem = 0

    def reduce_stage(first_sem, axis, count, me, src, dst, rows):
        copies = []
        for d in range(1, count):
            step = [0, 0, 0]
            step[axis] = d
            target = there(*step)
            start = pl.multiple_of(target[axis] * rows, 16)
            copy = pltpu.make_async_remote_copy(
                src_ref=src.at[pl.ds(start, rows)],
                dst_ref=dst.at[d - 1],
                send_sem=rs_send.at[first_sem + d - 1],
                recv_sem=rs_recv.at[first_sem + d - 1],
                device_id=target,
                device_id_type=MESH,
            )
            copy.start()
            copies.append(copy)
        return copies

    def own_share(src, me, rows, dst, copies):
        total = src[pl.ds(pl.multiple_of(me * rows, 16), rows), :]
        for d, copy in enumerate(copies):
            copy.wait_recv()
            total = total + dst[d].astype(F32)
        return total

    lat_rows = chunk * n_sec
    lon_rows = lat_rows * n_lat
    grad_b[...] = grad_ref[...].astype(BF16)
    copies = reduce_stage(sem, 2, n_lon, lon, grad_b, lon_in, lon_rows)
    sem += n_lon - 1
    waits += copies
    lon_sum[...] = own_share(grad_ref, lon, lon_rows, lon_in, copies)
    lon_b[...] = lon_sum[...].astype(BF16)
    copies = reduce_stage(sem, 1, n_lat, lat, lon_b, lat_in, lat_rows)
    sem += n_lat - 1
    waits += copies
    lat_sum[...] = own_share(lon_sum, lat, lat_rows, lat_in, copies)
    lat_b[...] = lat_sum[...].astype(BF16)
    copies = reduce_stage(sem, 0, n_sec, sec, lat_b, sec_in, chunk)
    waits += copies
    final = own_share(lat_sum, sec, chunk, sec_in, copies)
    gathered[lon, lat, sec] = final.astype(BF16)

    def gather_stage(first_sem, axis, count, view):
        copies = []
        for d in range(1, count):
            step = [0, 0, 0]
            step[axis] = d
            copy = pltpu.make_async_remote_copy(
                src_ref=view,
                dst_ref=view,
                send_sem=ag_send.at[first_sem + d - 1],
                recv_sem=ag_recv.at[first_sem + d - 1],
                device_id=there(*step),
                device_id_type=MESH,
            )
            copy.start()
            copies.append(copy)
        for copy in copies:
            copy.wait_recv()
        return copies

    waits += gather_stage(0, 1, n_lat, gathered.at[lon, lat, sec])
    waits += gather_stage(n_lat - 1, 2, n_lon, gathered.at[lon, :, sec])
    waits += gather_stage(n_lat + n_lon - 2, 0, n_sec, gathered.at[:, :, sec])

    whole = gathered[...].reshape(n_lon * n_lat * n_sec * chunk, 128).astype(F32) * factor

    def tile(t):
        return whole[t * WIDTH : (t + 1) * WIDTH]

    for t in range(4):
        g_qkv_ref[:, t * 128 : (t + 1) * 128] = tile(t)
    g_qkv_ref[:, 512:576] = tile(4)[:, :64]
    g_out_ref[...] = jnp.concatenate([tile(4), tile(5)], axis=1)[:, 64:256]
    for t in range(6):
        g_up_ref[:, t * 128 : (t + 1) * 128] = tile(6 + t)
        g_down_ref[:, t * 128 : (t + 1) * 128] = tile(12 + t)
    g_small_ref[...] = whole[18 * WIDTH : 18 * WIDTH + 8]

    for copy in waits:
        copy.wait_send()

    @pl.when(sec > 0)
    def _():
        cot_copy.wait_send()


def to_blocks(field):
    height, breadth, width = field.shape
    grid = field.reshape(height // 3, 3, breadth // 6, 6, width).transpose(2, 0, 1, 3, 4)
    grid = grid.reshape(breadth // 6, height // 3, HALF, width)
    grid = jnp.pad(grid, ((0, 0), (0, 0), (0, PAD - HALF), (0, 0)))
    return grid.reshape(-1, width)


def from_blocks(rows, height, breadth):
    width = rows.shape[-1]
    grid = rows.reshape(breadth // 6, height // 3, PAD, width)[:, :, :HALF]
    grid = grid.reshape(breadth // 6, height // 3, 3, 6, width).transpose(1, 2, 0, 3, 4)
    return grid.reshape(height, breadth, width)


def local(
    sizes,
    states,
    loss_grads,
    land_sea,
    land_embed,
    gain_attn,
    gain_mlp,
    w_qkv,
    w_out,
    w_up,
    w_down,
):
    n_sec, n_lat, n_lon = sizes
    height, breadth = states.shape[2:4]
    bands = height // WIN_LAT
    tokens = (height // 3) * (breadth // 6) * PAD
    half = tokens // 2
    window = 4 * PAD
    devices = n_sec * n_lat * n_lon
    used = 18 * WIDTH + 8
    chunk = 16 * (-(-used // (16 * devices)))
    total = chunk * devices
    factor = float(n_sec * height * n_lat * breadth * n_lon) ** (-0.5)
    vmem = pltpu.VMEM
    sds = jax.ShapeDtypeStruct
    wide = HEADS * window
    n_rs = (n_sec - 1) + (n_lat - 1) + (n_lon - 1)
    d_state, g_qkv, g_out, g_up, g_down, g_small = pl.pallas_call(
        functools.partial(kernel, sizes, bands, chunk, factor),
        out_shape=(
            sds((tokens, WIDTH), F32),
            sds((WIDTH, 3 * WIDTH), F32),
            sds((WIDTH, WIDTH), F32),
            sds((WIDTH, MLP), F32),
            sds((WIDTH, MLP), F32),
            sds((8, 128), F32),
        ),
        in_specs=[pl.BlockSpec(memory_space=vmem)] * 10,
        out_specs=[pl.BlockSpec(memory_space=vmem)] * 6,
        scratch_shapes=[
            vmem((4, tokens, WIDTH), BF16),
            vmem((4, 32, WIDTH), BF16),
            vmem((4, 32, WIDTH), BF16),
            vmem((4, half, WIDTH), BF16),
            vmem((bands, wide, WIDTH), BF16),
            vmem((tokens, WIDTH), BF16),
            vmem((tokens, WIDTH), BF16),
            vmem((bands, window, wide), F32),
            vmem((tokens, WIDTH), F32),
            vmem((tokens, WIDTH), F32),
            vmem((tokens, WIDTH), F32),
            vmem((tokens, WIDTH), BF16),
            vmem((tokens, WIDTH), BF16),
            vmem((tokens, MLP), F32),
            vmem((tokens, MLP), BF16),
            vmem((tokens, WIDTH), BF16),
            vmem((tokens, WIDTH), BF16),
            vmem((tokens, WIDTH), BF16),
            vmem((tokens, WIDTH), BF16),
            vmem((total, 128), F32),
            vmem((total, 128), BF16),
            vmem((n_lon - 1, total // n_lon, 128), BF16),
            vmem((total // n_lon, 128), F32),
            vmem((total // n_lon, 128), BF16),
            vmem((n_lat - 1, chunk * n_sec, 128), BF16),
            vmem((chunk * n_sec, 128), F32),
            vmem((chunk * n_sec, 128), BF16),
            vmem((n_sec - 1, chunk, 128), BF16),
            vmem((n_lon, n_lat, n_sec, chunk, 128), BF16),
            pltpu.SemaphoreType.DMA((4, 3)),
            pltpu.SemaphoreType.DMA((4, 3)),
            pltpu.SemaphoreType.DMA,
            pltpu.SemaphoreType.DMA,
            pltpu.SemaphoreType.DMA((n_rs,)),
            pltpu.SemaphoreType.DMA((n_rs,)),
            pltpu.SemaphoreType.DMA((n_rs,)),
            pltpu.SemaphoreType.DMA((n_rs,)),
        ],
        compiler_params=pltpu.CompilerParams(
            collective_id=0, has_side_effects=True, vmem_limit_bytes=48 * 1024 * 1024
        ),
    )(
        to_blocks(states[0, 0]),
        to_blocks(loss_grads[0, 0]),
        to_blocks(land_sea.astype(F32)[:, :, None]),
        land_embed[None],
        gain_attn[None],
        gain_mlp[None],
        w_qkv,
        w_out,
        w_up,
        w_down,
    )
    small = g_small[:6].reshape(3, 256)[:, :WIDTH]
    return (
        from_blocks(d_state, height, breadth)[None, None],
        g_qkv,
        g_out,
        g_up,
        g_down.T,
        small[0],
        small[1],
        small[2],
    )


def solution(mesh):
    sizes = tuple(mesh.shape[name] for name in ("section", "lat", "lon"))
    cells = P("section", None, "lat", "lon", None)
    return jax.shard_map(
        functools.partial(local, sizes),
        mesh=mesh,
        in_specs=(cells, cells, P("lat", "lon")) + (P(),) * 7,
        out_specs=(cells,) + (P(),) * 7,
        check_vma=False,
    )
```

```python
import functools

import jax
import jax.numpy as jnp
from jax import lax
from jax.experimental import pallas as pl
from jax.experimental.pallas import tpu as pltpu
from jax.sharding import PartitionSpec as P

HEADS = 6
HEAD_DIM = 32
WIN_LAT = 6
WIN_LON = 12
WIDTH = 192
MLP = 768
EPS = 1e-05

HALF = (WIN_LAT // 2) * (WIN_LON // 2)
PAD = 24
MESH = pl.DeviceIdType.MESH
F32 = jnp.float32
BF16 = jnp.bfloat16


def dot_nn(a, b):
    return jnp.dot(a, b, preferred_element_type=F32)


def dot_nt(a, b):
    return lax.dot_general(a, b, (((1,), (1,)), ((), ())), preferred_element_type=F32)


def dot_tn(a, b):
    return lax.dot_general(a, b, (((0,), (0,)), ((), ())), preferred_element_type=F32)


def mean_last(v):
    return jnp.sum(v, axis=-1, keepdims=True) * (1.0 / v.shape[-1])


def norm_parts(v):
    offset = v - mean_last(v)
    scale = lax.rsqrt(mean_last(offset * offset) + EPS)
    return offset * scale, scale


def norm_back(d_out, gain, hat, scale):
    d_hat = d_out * gain
    return scale * (d_hat - mean_last(d_hat) - hat * mean_last(d_hat * hat))


def head_masks():
    lane = lax.broadcasted_iota(jnp.int32, (1, WIDTH), 1)
    return [(lane >= h * HEAD_DIM) & (lane < (h + 1) * HEAD_DIM) for h in range(HEADS)]


def spread_heads(block, masks):
    return jnp.concatenate([jnp.where(m, block, 0.0) for m in masks], axis=0).astype(BF16)


def join_heads(stacked, masks):
    rows = stacked.shape[0] // HEADS
    total = jnp.where(masks[0], stacked[:rows], 0.0)
    for h in range(1, HEADS):
        total = jnp.where(masks[h], stacked[h * rows : (h + 1) * rows], total)
    return total


def interleave(first, second, bands):
    span = 2 * PAD
    parts = []
    for b in range(bands):
        parts += [first[b * span : (b + 1) * span], second[b * span : (b + 1) * span]]
    return jnp.concatenate(parts, axis=0)


def separate(field, bands):
    span = 2 * PAD
    firsts = [field[2 * b * span : (2 * b + 1) * span] for b in range(bands)]
    seconds = [field[(2 * b + 1) * span : (2 * b + 2) * span] for b in range(bands)]
    return jnp.concatenate(firsts + seconds, axis=0)


def kernel(
    sizes,
    bands,
    plan,
    field_ref,
    land_ref,
    embed_ref,
    ga_ref,
    gm_ref,
    wqkv_ref,
    wout_ref,
    wup_ref,
    wdown_ref,
    d_state_ref,
    g_qkv_ref,
    g_out_ref,
    g_up_ref,
    g_down_ref,
    g_small_ref,
    halo_src,
    halo_edge,
    halo_diag,
    halo_side,
    qm_ref,
    k_ref,
    v_ref,
    pt_ref,
    emb_hat,
    hid_hat,
    cot_ref,
    cot_src,
    cot_in,
    gelu_ref,
    act_ref,
    nmlp_ref,
    rolled_ref,
    mixed_ref,
    dqkv_ref,
    dproj_ref,
    dpre_ref,
    cotb_ref,
    grad_ref,
    grad_b,
    lon_in_a,
    lon_sum_a,
    lon_b_a,
    lat_in_a,
    lat_sum_a,
    lat_b_a,
    sec_in_a,
    gathered_a,
    lon_in_b,
    lon_sum_b,
    lon_b_b,
    lat_in_b,
    lat_sum_b,
    lat_b_b,
    sec_in_b,
    gathered_b,
    halo_send,
    halo_recv,
    cot_send,
    cot_recv,
    rs_send,
    rs_recv,
    ag_send,
    ag_recv,
):
    n_sec, n_lat, n_lon = sizes
    sec = lax.axis_index("section")
    lat = lax.axis_index("lat")
    lon = lax.axis_index("lon")

    def there(d_sec, d_lat, d_lon):
        return (
            lax.rem(sec + d_sec + n_sec, n_sec),
            lax.rem(lat + d_lat + n_lat, n_lat),
            lax.rem(lon + d_lon + n_lon, n_lon),
        )

    peers = [(d, 0, 0) for d in range(1, n_sec)]
    peers += [(0, d, 0) for d in range(1, n_lat)]
    peers += [(0, 0, d) for d in range(1, n_lon)]
    peers += [(0, 1, 1), (0, -1, -1)]
    barrier = pltpu.get_barrier_semaphore()
    for peer in peers:
        pl.semaphore_signal(barrier, inc=1, device_id=there(*peer), device_id_type=MESH)
    pl.semaphore_wait(barrier, len(peers))

    half = 2 * bands * PAD

    def halo(number, sign, edge_row, diag_row, side_row):
        copies = []
        for kind, (src, dst, target) in enumerate(
            (
                (halo_src.at[number, pl.ds(edge_row, 32)], halo_edge.at[number], (0, sign, 0)),
                (halo_src.at[number, pl.ds(diag_row, 32)], halo_diag.at[number], (0, sign, sign)),
                (halo_src.at[number, pl.ds(side_row, half)], halo_side.at[number], (0, 0, sign)),
            )
        ):
            copy = pltpu.make_async_remote_copy(
                src_ref=src,
                dst_ref=dst,
                send_sem=halo_send.at[number, kind],
                recv_sem=halo_recv.at[number, kind],
                device_id=there(*target),
                device_id_type=MESH,
            )
            copy.start()
            copies.append(copy)
        return copies

    def start_ahead(number, field):
        halo_src[number] = field.astype(BF16)
        return halo(number, -1, half, 0, 0)

    def end_ahead(number, copies):
        for copy in copies:
            copy.wait_recv()
        own = halo_src[number, pl.ds(half, half)].astype(F32)
        edge = halo_edge[number].astype(F32)
        diag = halo_diag[number].astype(F32)
        side = halo_side[number].astype(F32)
        first = jnp.concatenate([own[PAD:], edge[:PAD]], axis=0)
        second = jnp.concatenate([side[PAD:], diag[:PAD]], axis=0)
        return interleave(first, second, bands).astype(BF16)

    def start_behind(number, field):
        halo_src[number] = separate(field, bands).astype(BF16)
        return halo(number, 1, half - 32, 2 * half - 32, half)

    def end_behind(number, copies):
        for copy in copies:
            copy.wait_recv()
        own = halo_src[number, pl.ds(0, half)].astype(F32)
        edge = halo_edge[number].astype(F32)
        diag = halo_diag[number].astype(F32)
        side = halo_side[number].astype(F32)
        return jnp.concatenate(
            [diag[32 - PAD :], side[: half - PAD], edge[32 - PAD :], own[: half - PAD]], axis=0
        )

    masks = head_masks()
    window = 4 * PAD
    root = HEAD_DIM ** (-0.5)
    land = land_ref[...]
    gain_attn = ga_ref[...]
    gain_mlp = gm_ref[...]

    embedded = field_ref[0].astype(F32) + land * embed_ref[...]
    hat, emb_scale = norm_parts(embedded)
    emb_hat[...] = hat
    ahead_fwd = start_ahead(0, hat * gain_attn)

    key_id = lax.broadcasted_iota(jnp.int32, (window, HEADS * window), 0)
    query_id = lax.broadcasted_iota(jnp.int32, (window, HEADS * window), 1)
    for h in range(1, HEADS):
        query_id = jnp.where(
            lax.broadcasted_iota(jnp.int32, (window, HEADS * window), 1) >= h * window,
            lax.broadcasted_iota(jnp.int32, (window, HEADS * window), 1) - h * window,
            query_id,
        )

    def block_of(ids):
        return [ids >= n * PAD for n in range(1, 4)]

    k1, k2, k3 = block_of(key_id)
    q1, q2, q3 = block_of(query_id)
    key_start = jnp.where(k3, 3 * PAD, jnp.where(k2, 2 * PAD, jnp.where(k1, PAD, 0)))
    valid = jnp.where(key_id - key_start < HALF, 1.0, 0.0)
    key_late = jnp.where(k3, 1.0, jnp.where(k2, 0.0, jnp.where(k1, 1.0, 0.0)))
    query_late = jnp.where(q3, 1.0, jnp.where(q2, 0.0, jnp.where(q1, 1.0, 0.0)))
    differ = (key_late - query_late) * (key_late - query_late)
    wraps = jnp.where(lat == n_lat - 1, 1.0, 0.0)
    valid_edge = valid * (1.0 - differ * wraps)

    rolled = end_ahead(0, ahead_fwd)
    rolled_ref[...] = rolled
    w_q = wqkv_ref[:, 0:WIDTH]
    w_k = wqkv_ref[:, WIDTH : 2 * WIDTH]
    w_v = wqkv_ref[:, 2 * WIDTH : 3 * WIDTH]
    query = dot_nn(rolled, w_q)
    keys = dot_nn(rolled, w_k).astype(BF16)
    values = dot_nn(rolled, w_v).astype(BF16)
    k_ref[...] = keys
    v_ref[...] = values
    mixes = []
    for b in range(bands):
        rows = slice(b * window, (b + 1) * window)
        q_heads = spread_heads(query[rows], masks)
        qm_ref[b] = q_heads
        scores = dot_nt(keys[rows], q_heads) * root
        weights = jnp.exp(scores) * (valid_edge if b == bands - 1 else valid)
        probs = weights / jnp.sum(weights, axis=0, keepdims=True)
        pt_ref[b] = probs
        mixes.append(join_heads(dot_tn(probs.astype(BF16), values[rows]), masks))
    mixed = jnp.concatenate(mixes, axis=0).astype(BF16)
    mixed_ref[...] = mixed
    behind_fwd = start_behind(1, dot_nn(mixed, wout_ref[...]))

    hidden = embedded + end_behind(1, behind_fwd)
    hat2, hid_scale = norm_parts(hidden)
    hid_hat[...] = hat2
    normed_mlp = (hat2 * gain_mlp).astype(BF16)
    nmlp_ref[...] = normed_mlp
    pre = dot_nn(normed_mlp, wup_ref[...])
    cdf = 0.5 + 0.5 * lax.erf(pre * (0.5**0.5))
    act_ref[...] = (pre * cdf).astype(BF16)
    gelu_ref[...] = cdf + pre * (jnp.exp(pre * pre * -0.5) * 0.3989422804014327)

    cot_ref[...] = field_ref[1].astype(F32)
    cot_copy = pltpu.make_async_remote_copy(
        src_ref=cot_src,
        dst_ref=cot_in,
        send_sem=cot_send,
        recv_sem=cot_recv,
        device_id=there(-1, 0, 0),
        device_id_type=MESH,
    )

    @pl.when(sec < n_sec - 1)
    def _():
        cot_copy.wait_recv()
        cot_ref[...] += cot_in[...].astype(F32)

    cot = cot_ref[...]
    cot_round = cot.astype(BF16)
    d_pre = (gelu_ref[...] * dot_nt(cot_round, wdown_ref[...])).astype(BF16)
    d_nmlp = dot_nt(d_pre, wup_ref[...])
    d_hidden = cot + norm_back(d_nmlp, gain_mlp, hid_hat[...], hid_scale)
    ahead_bwd = start_ahead(2, d_hidden)

    base_b, split, chunks = plan
    row_bases = (0, base_b)
    bufs = (
        (lon_in_a, lon_sum_a, lon_b_a, lat_in_a, lat_sum_a, lat_b_a, sec_in_a, gathered_a),
        (lon_in_b, lon_sum_b, lon_b_b, lat_in_b, lat_sum_b, lat_b_b, sec_in_b, gathered_b),
    )
    axes = ((2, n_lon, lon), (1, n_lat, lat), (0, n_sec, sec))

    def put_rows(start, block):
        end = start + block.shape[0]
        if start < split:
            stop = min(end, split)
            grad_ref[start:stop, :] = block[: stop - start]
        if end > split:
            begin = max(start, split)
            place = base_b + begin - split
            grad_ref[place : place + end - begin, :] = block[begin - start :]

    def put_tiles(first, block):
        for t in range(block.shape[1] // 128):
            put_rows((first + t) * WIDTH, block[:, t * 128 : (t + 1) * 128])

    def put_small(index, vector):
        row = base_b + 18 * WIDTH - split + 2 * index
        grad_ref[row : row + 1, :] = vector[:, :128]
        grad_ref[row + 1 : row + 2, 0:64] = vector[:, 128:WIDTH]

    def share_rows(part, stage):
        rows = chunks[part]
        for _, count, _ in axes[stage + 1 :]:
            rows *= count
        return rows

    def reduce_copies(part, stage):
        src = (grad_b, bufs[part][2], bufs[part][5])[stage]
        dst = (bufs[part][0], bufs[part][3], bufs[part][6])[stage]
        base = row_bases[part] if stage == 0 else 0
        rows = share_rows(part, stage)
        axis, count, _ = axes[stage]
        first_sem = sum(n - 1 for _, n, _ in axes[:stage])
        copies = []
        for d in range(1, count):
            step = [0, 0, 0]
            step[axis] = d
            target = there(*step)
            start = pl.multiple_of(base + target[axis] * rows, 16)
            copies.append(
                pltpu.make_async_remote_copy(
                    src_ref=src.at[pl.ds(start, rows)],
                    dst_ref=dst.at[d - 1],
                    send_sem=rs_send.at[part, first_sem + d - 1],
                    recv_sem=rs_recv.at[part, first_sem + d - 1],
                    device_id=target,
                    device_id_type=MESH,
                )
            )
        return copies

    def start_lon(part):
        rows = share_rows(part, 0) * n_lon
        span = slice(row_bases[part], row_bases[part] + rows)
        grad_b[span, :] = grad_ref[span, :].astype(BF16)
        for copy in reduce_copies(part, 0):
            copy.start()

    def own_share(part, stage):
        src = (grad_ref, bufs[part][1], bufs[part][4])[stage]
        dst = (bufs[part][0], bufs[part][3], bufs[part][6])[stage]
        base = row_bases[part] if stage == 0 else 0
        rows = share_rows(part, stage)
        total = src[pl.ds(pl.multiple_of(base + axes[stage][2] * rows, 16), rows), :]
        for d, copy in enumerate(reduce_copies(part, stage)):
            copy.wait_recv()
            total = total + dst[d].astype(F32)
        return total

    def next_stage(part, stage):
        total = own_share(part, stage)
        if stage == 2:
            bufs[part][7][lon, lat, sec] = total.astype(BF16)
            return
        bufs[part][1 + 3 * stage][...] = total
        bufs[part][2 + 3 * stage][...] = total.astype(BF16)
        for copy in reduce_copies(part, stage + 1):
            copy.start()

    def gather_copies(part, stage):
        gathered = bufs[part][7]
        own = (sec, lat, lon)
        first_sem = (0, n_lat - 1, n_lat + n_lon - 2, n_lat + n_lon)[stage]
        if stage == 0:
            view = gathered.at[lon, lat, sec]
            targets = [there(0, d, 0) for d in range(1, n_lat)]
        elif stage == 1:
            view = gathered.at[lon, :, sec]
            targets = [there(0, 0, d) for d in range(1, n_lon)]
        elif n_sec != 4:
            view = gathered.at[:, :, sec]
            targets = [there(d, 0, 0) for d in range(1, n_sec)] if stage == 2 else []
        else:
            sibling = (sec + 1 - 2 * lax.rem(sec, 2), own[1], own[2])
            across = there(2, 0, 0)
            view = gathered.at[:, :, sec if stage == 2 else across[0]]
            targets = [across, sibling] if stage == 2 else [sibling]
        return [
            pltpu.make_async_remote_copy(
                src_ref=view,
                dst_ref=view,
                send_sem=ag_send.at[part, first_sem + n],
                recv_sem=ag_recv.at[part, first_sem + n],
                device_id=target,
                device_id_type=MESH,
            )
            for n, target in enumerate(targets)
        ]

    def start_gather(part, stage):
        for copy in gather_copies(part, stage):
            copy.start()

    def end_gather(part, stage):
        for copy in gather_copies(part, stage):
            copy.wait_recv()

    tail = base_b + 18 * WIDTH - split
    grad_ref[tail:, :] = jnp.zeros((grad_ref.shape[0] - tail, 128), F32)
    if split < base_b:
        grad_ref[split:base_b, :] = jnp.zeros((base_b - split, 128), F32)
    dpre_ref[...] = d_pre
    cotb_ref[...] = cot_round

    def mlp_grads():
        put_tiles(0, dot_tn(nmlp_ref[...], dpre_ref[...]))
        put_tiles(6, dot_tn(cotb_ref[...], act_ref[...]))
        start_lon(0)

    @pl.when(sec == 0)
    def _():
        mlp_grads()

    put_small(2, jnp.sum(d_nmlp * hid_hat[...], axis=0, keepdims=True))

    d_projected = end_ahead(2, ahead_bwd)
    d_mixed = dot_nt(d_projected, wout_ref[...])
    d_queries, d_keys, d_values = [], [], []
    for b in range(bands):
        rows = slice(b * window, (b + 1) * window)
        d_heads = spread_heads(d_mixed[rows], masks)
        probs = pt_ref[b]
        d_probs = dot_nt(v_ref[rows, :], d_heads)
        weighted = probs * d_probs
        d_scores = (
            (weighted - probs * jnp.sum(weighted, axis=0, keepdims=True)) * root
        ).astype(BF16)
        d_values.append(dot_nn(probs.astype(BF16), d_heads))
        d_keys.append(dot_nn(d_scores, qm_ref[b]))
        d_queries.append(join_heads(dot_tn(d_scores, k_ref[rows, :]), masks))
    d_q = jnp.concatenate(d_queries, axis=0).astype(BF16)
    d_k = jnp.concatenate(d_keys, axis=0).astype(BF16)
    d_v = jnp.concatenate(d_values, axis=0).astype(BF16)
    d_rolled = dot_nt(d_q, w_q) + dot_nt(d_k, w_k) + dot_nt(d_v, w_v)
    behind_bwd = start_behind(3, d_rolled)

    dproj_ref[...] = d_projected
    dqkv_ref[0] = d_q
    dqkv_ref[1] = d_k
    dqkv_ref[2] = d_v

    def attn_grads():
        rolled = rolled_ref[...]
        g_q, g_k, g_v = (dot_tn(rolled, dqkv_ref[n]) for n in range(3))
        put_tiles(12, jnp.concatenate([g_q, g_k], axis=1))
        g_o = dot_tn(mixed_ref[...], dproj_ref[...])
        put_tiles(15, jnp.concatenate([g_v, g_o], axis=1))
        next_stage(0, 0)

    @pl.when(sec == 0)
    def _():
        attn_grads()

    d_normed = end_behind(3, behind_bwd)
    hat = emb_hat[...]
    d_state = d_hidden + norm_back(d_normed, gain_attn, hat, emb_scale)
    cot_src[...] = d_state.astype(BF16)

    @pl.when(sec > 0)
    def _():
        cot_copy.start()
        mlp_grads()
        attn_grads()

    d_state_ref[...] = d_state
    put_small(0, jnp.sum(d_state * land, axis=0, keepdims=True))
    put_small(1, jnp.sum(d_normed * hat, axis=0, keepdims=True))

    start_lon(1)
    next_stage(0, 1)
    next_stage(1, 0)
    next_stage(0, 2)
    start_gather(0, 0)
    next_stage(1, 1)
    end_gather(0, 0)
    start_gather(0, 1)
    next_stage(1, 2)
    start_gather(1, 0)
    end_gather(0, 1)
    start_gather(0, 2)
    end_gather(1, 0)
    start_gather(1, 1)
    end_gather(1, 1)
    start_gather(1, 2)
    end_gather(0, 2)
    start_gather(0, 3)
    end_gather(1, 2)
    start_gather(1, 3)
    end_gather(0, 3)
    whole_a = gathered_a[...].reshape(-1, 128)[:split]
    end_gather(1, 3)
    whole_b = gathered_b[...].reshape(-1, 128)

    def tile(t):
        start, end = t * WIDTH, (t + 1) * WIDTH
        if end <= split:
            return whole_a[start:end]
        if start >= split:
            return whole_b[start - split : end - split]
        return jnp.concatenate([whole_a[start:], whole_b[: end - split]], axis=0)

    for t in range(6):
        g_up_ref[:, t * 128 : (t + 1) * 128] = tile(t)
        g_down_ref[:, t * 128 : (t + 1) * 128] = tile(6 + t)
    for t in range(4):
        g_qkv_ref[:, t * 128 : (t + 1) * 128] = tile(12 + t)
    g_qkv_ref[:, 512:576] = tile(16)[:, :64]
    last = jnp.concatenate([tile(16), tile(17)], axis=1).astype(F32)
    g_out_ref[...] = last[:, 64:256].astype(BF16)
    small = 18 * WIDTH - split
    g_small_ref[...] = whole_b[small : small + 16].astype(F32)

    for copy in ahead_fwd + behind_fwd + ahead_bwd + behind_bwd:
        copy.wait_send()
    for part in range(2):
        for stage in range(3):
            for copy in reduce_copies(part, stage):
                copy.wait_send()
        for stage in range(4):
            for copy in gather_copies(part, stage):
                copy.wait_send()

    @pl.when(sec > 0)
    def _():
        cot_copy.wait_send()


def to_blocks(field):
    count, height, breadth, width = field.shape
    grid = field.reshape(count, height // 3, 3, breadth // 6, 6, width)
    grid = grid.transpose(0, 3, 1, 2, 4, 5)
    grid = grid.reshape(count, breadth // 6, height // 3, HALF, width)
    grid = jnp.pad(grid, ((0, 0), (0, 0), (0, 0), (0, PAD - HALF), (0, 0)))
    return grid.reshape(count, -1, width)


def from_blocks(rows, height, breadth):
    width = rows.shape[-1]
    grid = rows.reshape(breadth // 6, height // 3, PAD, width)[:, :, :HALF]
    grid = grid.reshape(breadth // 6, height // 3, 3, 6, width).transpose(1, 2, 0, 3, 4)
    return grid.reshape(height, breadth, width)


def reduce_scratch(chunk, sizes):
    n_sec, n_lat, n_lon = sizes
    lat_rows = chunk * n_sec
    lon_rows = lat_rows * n_lat
    return [
        pltpu.VMEM((n_lon - 1, lon_rows, 128), BF16),
        pltpu.VMEM((lon_rows, 128), F32),
        pltpu.VMEM((lon_rows, 128), BF16),
        pltpu.VMEM((n_lat - 1, lat_rows, 128), BF16),
        pltpu.VMEM((lat_rows, 128), F32),
        pltpu.VMEM((lat_rows, 128), BF16),
        pltpu.VMEM((n_sec - 1, chunk, 128), BF16),
        pltpu.VMEM((n_lon, n_lat, n_sec, chunk, 128), BF16),
    ]


def local(
    sizes,
    states,
    loss_grads,
    land_sea,
    land_embed,
    gain_attn,
    gain_mlp,
    w_qkv,
    w_out,
    w_up,
    w_down,
):
    n_sec, n_lat, n_lon = sizes
    height, breadth = states.shape[2:4]
    bands = height // WIN_LAT
    tokens = (height // 3) * (breadth // 6) * PAD
    half = tokens // 2
    window = 4 * PAD
    devices = n_sec * n_lat * n_lon
    unit = 16 * devices
    mlp_rows = 12 * WIDTH
    units_a = max(1, mlp_rows // unit)
    split = min(mlp_rows, units_a * unit)
    units_b = -(-(18 * WIDTH + 16 - split) // unit)
    chunks = (16 * units_a, 16 * units_b)
    plan = (units_a * unit, split, chunks)
    total = (units_a + units_b) * unit
    factor = float(n_sec * height * n_lat * breadth * n_lon) ** (-0.5)
    vmem = pltpu.VMEM
    sds = jax.ShapeDtypeStruct
    wide = HEADS * window
    n_rs = (n_sec - 1) + (n_lat - 1) + (n_lon - 1)
    d_state, g_qkv, g_out, g_up, g_down, g_small = pl.pallas_call(
        functools.partial(kernel, sizes, bands, plan),
        out_shape=(
            sds((tokens, WIDTH), F32),
            sds((WIDTH, 3 * WIDTH), BF16),
            sds((WIDTH, WIDTH), BF16),
            sds((WIDTH, MLP), BF16),
            sds((WIDTH, MLP), BF16),
            sds((16, 128), F32),
        ),
        in_specs=[pl.BlockSpec(memory_space=vmem)] * 9,
        out_specs=[pl.BlockSpec(memory_space=vmem)] * 6,
        scratch_shapes=[
            vmem((4, tokens, WIDTH), BF16),
            vmem((4, 32, WIDTH), BF16),
            vmem((4, 32, WIDTH), BF16),
            vmem((4, half, WIDTH), BF16),
            vmem((bands, wide, WIDTH), BF16),
            vmem((tokens, WIDTH), BF16),
            vmem((tokens, WIDTH), BF16),
            vmem((bands, window, wide), F32),
            vmem((tokens, WIDTH), F32),
            vmem((tokens, WIDTH), F32),
            vmem((tokens, WIDTH), F32),
            vmem((tokens, WIDTH), BF16),
            vmem((tokens, WIDTH), BF16),
            vmem((tokens, MLP), F32),
            vmem((tokens, MLP), BF16),
            vmem((tokens, WIDTH), BF16),
            vmem((tokens, WIDTH), BF16),
            vmem((tokens, WIDTH), BF16),
            vmem((3, tokens, WIDTH), BF16),
            vmem((tokens, WIDTH), BF16),
            vmem((tokens, MLP), BF16),
            vmem((tokens, WIDTH), BF16),
            vmem((total, 128), F32),
            vmem((total, 128), BF16),
            *reduce_scratch(chunks[0], sizes),
            *reduce_scratch(chunks[1], sizes),
            pltpu.SemaphoreType.DMA((4, 3)),
            pltpu.SemaphoreType.DMA((4, 3)),
            pltpu.SemaphoreType.DMA,
            pltpu.SemaphoreType.DMA,
            pltpu.SemaphoreType.DMA((2, n_rs)),
            pltpu.SemaphoreType.DMA((2, n_rs)),
            pltpu.SemaphoreType.DMA((2, n_rs)),
            pltpu.SemaphoreType.DMA((2, n_rs)),
        ],
        compiler_params=pltpu.CompilerParams(
            collective_id=0, has_side_effects=True, vmem_limit_bytes=48 * 1024 * 1024
        ),
    )(
        to_blocks(jnp.concatenate([states[0], loss_grads[0]])),
        to_blocks(land_sea.astype(F32)[None, :, :, None])[0],
        land_embed[None],
        gain_attn[None],
        gain_mlp[None],
        w_qkv,
        w_out,
        w_up,
        w_down,
    )
    small = g_small[:6].reshape(3, 256)[:, :WIDTH] * factor
    return (
        from_blocks(d_state, height, breadth)[None, None],
        g_qkv.astype(F32) * factor,
        g_out.astype(F32) * factor,
        g_up.astype(F32) * factor,
        g_down.T.astype(F32) * factor,
        small[0],
        small[1],
        small[2],
    )


def solution(mesh):
    sizes = tuple(mesh.shape[name] for name in ("section", "lat", "lon"))
    cells = P("section", None, "lat", "lon", None)
    return jax.shard_map(
        functools.partial(local, sizes),
        mesh=mesh,
        in_specs=(cells, cells, P("lat", "lon")) + (P(),) * 7,
        out_specs=(cells,) + (P(),) * 7,
        check_vma=False,
    )
```
